32 devices in a mesh: groups: 1, user: 16 (over z, y, x), item: 2 (over core).
Axes of the slice: x: 2, y: 2, z: 4, core: 2. Of those that a mesh axis runs over, the one named last changes fastest.
Arguments:
- blocks: bfloat16 [14336, 16, 256], P(('groups', 'user', 'item')), may hold values from -12 to 12
- user_blocks: int32 [14336], P(('groups', 'user', 'item')), may hold values from 0 to 127, as said below
- item_blocks: int32 [14336], P(('groups', 'user', 'item')), may hold values from 0 to 31, as said below
- time_blocks: int32 [14336], P(('groups', 'user', 'item')), may hold values from 0 to 15
- block_counts: int32 [32], P(('groups', 'user', 'item')), may hold values from 28 to 448, as said below
- item_factor: bfloat16 [512, 256], P(('groups', 'user', 'item')), may hold values from -0.25 to 0.25
- item_previous: bfloat16 [512, 256], P(('groups', 'user', 'item')), may hold values from -0.25 to 0.25
- time_factor: bfloat16 [256, 256], P(('groups', 'user')), may hold values from -0.375 to 0.375
- time_previous: bfloat16 [256, 256], P(('groups', 'user')), may hold values from -0.375 to 0.375
Outputs:
- row_products: float32 [2, 2048, 256], P(None, ('groups', 'user', 'item'))
- hadamard_grams: float32 [2, 256, 256], P('groups')
The draws below stay inside these ranges and needn't reach their ends.
Inputs may be any that keep to these rules, and one draw needn't show every extreme that they name: `block_counts`: the live slots of a device come first among its 448 slots; some device has 448 of them and another 448 // 16. `user_blocks`: A slot of device d (slot index div 448) names a user block of range d div 2: its index lies from (d div 2) * 64 * 2 // 16 up to one range further. `item_blocks`: A slot of device d names an item block that lies in the item factor rows of some device e with e mod 2 = d mod 2 (rows e * 16 to (e + 1) * 16 - 1).
All inputs are finite; a program needn't handle non-finite values.
Results may differ from the reference program's by a relative error of at most 0.0049.
Values may be sent and summed in bfloat16 or wider, within the bound.
A program may use at most 64 MiB of HBM per device.

```python
import jax
import jax.numpy as jnp
from jax import lax

R = 256
BS = 16
NB_CAP = 448
U_DEV = 64
I_SH = 16
HOLDERS = 32
NBT = 14336
U = 2048
I = 512
TM = 256
N_USER = 16
N_ITEM = 2


def draw_block_counts(key, part):
    key = jax.random.fold_in(key, 7)
    holders = N_USER * N_ITEM
    key_level, key_top, key_low = jax.random.split(key, 3)
    level = jax.random.randint(key_level, (holders,), 4, 17)
    top_place = jax.random.randint(key_top, (), 0, holders)
    low_place = (top_place + 1 + jax.random.randint(key_low, (), 0, holders - 1)) % holders
    places = jnp.arange(holders, dtype=jnp.int32)
    level = jnp.where(places == top_place, 16, jnp.where(places == low_place, 4, level))
    return (NB_CAP * level * level // 256).astype(jnp.int32)


def draw_user_blocks(key, part):
    key = jax.random.fold_in(key, 11)
    total = NB_CAP * N_USER * N_ITEM
    owner = jnp.arange(total, dtype=jnp.int32) // NB_CAP
    span = U_DEV * N_ITEM // BS
    offset = jax.random.randint(key, (total,), 0, span)
    return (owner // N_ITEM * span + offset).astype(jnp.int32)


def draw_item_blocks(key, part):
    key = jax.random.fold_in(key, 13)
    key_shard, key_off = jax.random.split(key)
    total = NB_CAP * N_USER * N_ITEM
    owner = jnp.arange(total, dtype=jnp.int32) // NB_CAP
    per_shard = I_SH // BS
    column = jax.random.randint(key_shard, (total,), 0, N_USER)
    offset = jax.random.randint(key_off, (total,), 0, per_shard)
    shard = column * N_ITEM + owner % N_ITEM
    return (shard * per_shard + offset).astype(jnp.int32)


def plant(entries, rng, smallest, top_value):
    extent = entries.shape
    index_at = [jax.random.randint(jax.random.fold_in(rng, axis), (), 0, extent[axis]) for axis in range(len(extent))]
    entries = entries.at[tuple(index_at)].set(smallest)
    longest = extent.index(max(extent))
    index_at[longest] = (index_at[longest] + 1) % extent[longest]
    return entries.at[tuple(index_at)].set(top_value)


def block_levels(stream_key, extent, pieces, low, top_value):
    level = 1.0
    for axis_at, parts in pieces:
        draws = jax.random.uniform(jax.random.fold_in(jax.random.fold_in(stream_key, 6), axis_at), (parts,), jnp.float32, low / len(pieces), top_value / len(pieces))
        level = level * jnp.repeat(jnp.exp(draws), extent[axis_at] // parts).reshape((-1,) + (1,) * (len(extent) - 1 - axis_at))
    return level


def noise(rng, extent, scale, limit, pieces=(), kind=jnp.bfloat16):
    level = block_levels(rng, extent, pieces, -0.22, 0.18) if pieces else 1.0
    result = jax.random.normal(rng, extent, jnp.float32) * scale * level
    return jnp.minimum(jnp.maximum(result, -limit), limit).astype(kind)


def setup_inputs(seed: int = 0, part: int = 0) -> dict:
    splits = jax.random.split(jax.random.key(seed), 10)
    own_keys = jax.random.split(jax.random.fold_in(splits[9], part), 10)
    return {
        "blocks": noise(own_keys[0], (NBT, BS, BS * BS), 2.0, 12.0, ((0, 32),)),
        "user_blocks": draw_user_blocks(jax.random.fold_in(jax.random.fold_in(splits[9], part), 71), part),
        "item_blocks": draw_item_blocks(jax.random.fold_in(jax.random.fold_in(splits[9], part), 71), part),
        "time_blocks": plant(jax.random.randint(own_keys[3], (NBT,), 0, TM // BS), jax.random.fold_in(own_keys[3], 1), 0, (TM // BS) - 1).astype(jnp.int32),
        "block_counts": draw_block_counts(jax.random.fold_in(jax.random.fold_in(splits[9], part), 71), part),
        "item_factor": noise(own_keys[5], (I, R), I ** -0.5, 0.25, ((0, 32),)),
        "item_previous": noise(own_keys[6], (I, R), I ** -0.5, 0.25, ((0, 32),)),
        "time_factor": noise(own_keys[7], (TM, R), TM ** -0.5, 0.375, ((0, 16),)),
        "time_previous": noise(own_keys[8], (TM, R), TM ** -0.5, 0.375, ((0, 16),)),
    }


extrapolation = 0.5


def extended(current, previous):
    wide_now = current.astype(jnp.float32)
    grown = wide_now + extrapolation * (wide_now - previous.astype(jnp.float32))
    return grown.astype(jnp.bfloat16)


def reference(blocks, user_blocks, item_blocks, time_blocks, block_counts, item_factor, item_previous, time_factor, time_previous):
    item_sets = jnp.stack([item_factor, extended(item_factor, item_previous)])
    time_sets = jnp.stack([time_factor, extended(time_factor, time_previous)])
    item_tiles = item_sets.reshape(2, -1, BS, R)
    time_tiles = time_sets.reshape(2, -1, BS, R)
    alive_all = jnp.arange(NB_CAP, dtype=jnp.int32)[None, :] < block_counts[:, None]
    values = blocks.reshape(HOLDERS, NB_CAP, BS, BS * BS)
    users = user_blocks.reshape(HOLDERS, NB_CAP)
    items = item_blocks.reshape(HOLDERS, NB_CAP)
    times = time_blocks.reshape(HOLDERS, NB_CAP)

    def visit(total, inputs):
        tensor, alive, user_index, item_index, time_index = inputs
        tensor = jnp.where(alive[:, None, None], tensor, jnp.zeros_like(tensor))
        left = item_tiles[:, item_index].astype(jnp.float32)
        right = time_tiles[:, time_index].astype(jnp.float32)
        khatri = (left[:, :, :, None, :] * right[:, :, None, :, :]).astype(jnp.bfloat16)
        khatri = lax.optimization_barrier(khatri)
        khatri = khatri.reshape(2, NB_CAP, BS * BS, R).astype(jnp.float32)
        part = jnp.einsum("gaq,sgqr->gasr", tensor.astype(jnp.float32), khatri, precision=lax.Precision.HIGHEST)
        return total + jax.ops.segment_sum(part, user_index, num_segments=U // BS), jnp.float32(0.0)

    empty = jnp.zeros((U // BS, BS, 2, R), jnp.float32)
    total, unused = lax.scan(visit, empty, (values, alive_all, users, items, times))
    row_products = total.reshape(U, 2, R).transpose(1, 0, 2)
    item_wide = item_sets.astype(jnp.float32)
    time_wide = time_sets.astype(jnp.float32)
    item_gram = jnp.einsum("sir,sic->src", item_wide, item_wide, precision=lax.Precision.HIGHEST)
    time_gram = jnp.einsum("sir,sic->src", time_wide, time_wide, precision=lax.Precision.HIGHEST)
    return row_products, item_gram * time_gram
```

```python
import functools

import jax
import jax.numpy as jnp
from jax import lax
from jax.experimental import pallas as pl
from jax.experimental.pallas import tpu as pltpu
from jax.sharding import PartitionSpec as P

BS = 16
U_DEV = 64
LANE = 128
WIDTH = 4
UNROLL = 4
DEAD = 1 << 28

extrapolation = 0.5


def extended(current, previous):
    wide_now = current.astype(jnp.float32)
    grown = wide_now + extrapolation * (wide_now - previous.astype(jnp.float32))
    return grown.astype(jnp.bfloat16)


def as_columns(row, size):
    parts = []
    for at in range(0, size, LANE):
        square = jnp.broadcast_to(row[:, at : at + LANE], (LANE, LANE))
        parts.append(square.T)
    return jnp.concatenate(parts, axis=0)


def plan_groups(key, value, table_ref):
    size = key.shape[1]
    down = lax.broadcasted_iota(jnp.int32, (size, LANE), 0)
    across = lax.broadcasted_iota(jnp.int32, (1, LANE), 1)
    chunks = [slice(at, at + LANE) for at in range(0, size, LANE)]
    key_col = as_columns(key, size)
    places = []
    for n, cut in enumerate(chunks):
        earlier = (key_col == key[:, cut]) & (down < across + n * LANE)
        places.append(jnp.sum(earlier.astype(jnp.int32), axis=0, keepdims=True))
    place = jnp.concatenate(places, axis=1)
    alive = key < DEAD
    order = jnp.where(alive, key * size + place, jnp.int32(2**31 - 1))
    order_col = as_columns(order, size)
    leads = (order_col & (WIDTH - 1)) == 0
    groups = []
    for cut in chunks:
        ahead = leads & (order_col <= order[:, cut])
        groups.append(jnp.sum(ahead.astype(jnp.int32), axis=0, keepdims=True))
    group = jnp.concatenate(groups, axis=1) - 1
    spot = jnp.where(alive, group * WIDTH + (place & (WIDTH - 1)), -1)
    spot_col = as_columns(spot, size)
    value_col = as_columns(value, size)
    zero = jnp.zeros_like(key_col)
    table_ref[...] = jnp.zeros(table_ref.shape, jnp.int32)
    for n, cut in enumerate(chunks):
        base = (across + n * LANE) * WIDTH
        for m in range(WIDTH):
            here = spot_col == base + m
            picked = jnp.sum(jnp.where(here, value_col, zero), axis=0, keepdims=True)
            table_ref[m : m + 1, cut] = picked
            if m == 0:
                keys = jnp.sum(jnp.where(here, key_col, zero), axis=0, keepdims=True)
                table_ref[WIDTH : WIDTH + 1, cut] = keys
    total = jnp.sum(leads.astype(jnp.int32), axis=0, keepdims=True)
    table_ref[WIDTH + 1 : WIDTH + 2, 0:LANE] = total


def gather_kernel(
    n_user, key_ref, value_ref, item_ref, item_old_ref, time_ref, time_old_ref,
    items_ref, times_ref, table_ref, own, held, send_sem, recv_sem,
):
    me = lax.axis_index("user")
    rows_i, rows_t = item_ref.shape[0], time_ref.shape[0]
    barrier = pltpu.get_barrier_semaphore()

    def greet(d, carry):
        peer = lax.rem(me + d, n_user)
        pl.semaphore_signal(barrier, inc=1, device_id={"user": peer}, device_id_type=pl.DeviceIdType.MESH)
        return carry

    lax.fori_loop(1, n_user, greet, 0)
    own[0:rows_i] = item_ref[...]
    own[rows_i : 2 * rows_i] = extended(item_ref[...], item_old_ref[...])
    own[2 * rows_i : 2 * rows_i + rows_t] = time_ref[...]
    own[2 * rows_i + rows_t :] = extended(time_ref[...], time_old_ref[...])
    pl.semaphore_wait(barrier, n_user - 1)

    def copy(d, slot, peer):
        return pltpu.make_async_remote_copy(
            src_ref=own, dst_ref=held.at[slot], send_sem=send_sem.at[d], recv_sem=recv_sem.at[d],
            device_id={"user": peer}, device_id_type=pl.DeviceIdType.MESH,
        )

    def send(d, carry):
        copy(d, me, lax.rem(me + d, n_user)).start()
        return carry

    lax.fori_loop(1, n_user, send, 0)
    plan_groups(key_ref[...], value_ref[...], table_ref)

    def place(source, block):
        at_i = pl.multiple_of(source * rows_i, rows_i)
        at_t = pl.multiple_of(source * rows_t, rows_t)
        for s in range(2):
            items_ref[s, pl.ds(at_i, rows_i)] = block[s * rows_i : (s + 1) * rows_i]
            low = 2 * rows_i + s * rows_t
            times_ref[s, pl.ds(at_t, rows_t)] = block[low : low + rows_t]

    place(me, own)

    def take(d, carry):
        source = lax.rem(me - d + n_user, n_user)
        copy(d, source, source).wait_recv()
        place(source, held.at[source])
        return carry

    lax.fori_loop(1, n_user, take, 0)

    def sent(d, carry):
        copy(d, me, lax.rem(me + d, n_user)).wait_send()
        return carry

    lax.fori_loop(1, n_user, sent, 0)


def product_kernel(shift, table_ref, items_ref, times_ref, blocks_ref, part_ref, tensor, spread, acc, sem):
    rank = items_ref.shape[2]
    load = pltpu.make_async_copy(blocks_ref, tensor, sem)
    load.start()
    acc[...] = jnp.zeros_like(acc)

    def widen(tile, carry):
        at = pl.multiple_of(tile * BS, BS)
        for s in range(2):
            rows = items_ref[s, pl.ds(at, BS)].astype(jnp.float32)
            for j in range(BS):
                wide = jnp.broadcast_to(rows[j : j + 1], (BS, rank))
                spread[s, tile, j * BS : (j + 1) * BS] = wide.astype(jnp.bfloat16)
        return carry

    lax.fori_loop(0, items_ref.shape[1] // BS, widen, 0)
    load.wait()
    count = table_ref[WIDTH + 1, 0]

    def turn(g, carry):
        for v in range(UNROLL):
            c = g * UNROLL + v
            key = table_ref[WIDTH, c]
            tile = key >> shift
            at = pl.multiple_of((key & ((1 << shift) - 1)) * BS, BS)
            member = [table_ref[m, c] for m in range(WIDTH)]
            x = jnp.concatenate([tensor[word >> 4] for word in member], axis=0)
            for s in range(2):
                right = times_ref[s, pl.ds(at, BS)]
                left = spread[s, tile].reshape(BS, BS, rank)
                khatri = (left * right[None]).reshape(BS * BS, rank)
                y = jnp.dot(x, khatri, preferred_element_type=jnp.float32)
                for m, word in enumerate(member):
                    acc[s, word & 15] += y[m * BS : (m + 1) * BS]
        return carry

    lax.fori_loop(0, (count + UNROLL - 1) // UNROLL, turn, 0)
    tiles = U_DEV // BS
    for half in range(part_ref.shape[0]):
        for s in range(2):
            for n in range(tiles):
                part_ref[half, s, n * BS : (n + 1) * BS] = acc[s, 1 + half * tiles + n]


def gram(rows):
    return lax.dot_general(rows, rows, (((0,), (0,)), ((), ())), preferred_element_type=jnp.float32)


def finish_kernel(part_ref, items_ref, times_ref, rows_ref, grams_ref, theirs, items, send_sem, recv_sem):
    me = lax.axis_index("item")
    other = 1 - me
    barrier = pltpu.get_barrier_semaphore()
    pl.semaphore_signal(barrier, inc=1, device_id={"item": other}, device_id_type=pl.DeviceIdType.MESH)
    pl.semaphore_wait(barrier, 1)
    copies = []
    for n, (src, dst) in enumerate(((part_ref.at[other], theirs), (items_ref, items))):
        copies.append(
            pltpu.make_async_remote_copy(
                src_ref=src, dst_ref=dst, send_sem=send_sem.at[n], recv_sem=recv_sem.at[n],
                device_id={"item": other}, device_id_type=pl.DeviceIdType.MESH,
            )
        )
        copies[-1].start()
    mine = [gram(items_ref[s]) for s in range(2)]
    times = [gram(times_ref[s]) for s in range(2)]
    copies[0].wait()
    rows_ref[...] = part_ref[me] + theirs[...]
    copies[1].wait()
    for s in range(2):
        grams_ref[s] = (mine[s] + gram(items[s])) * times[s]


def local(
    n_user, n_item, blocks, user_blocks, item_blocks, time_blocks, block_counts,
    item_factor, item_previous, time_factor, time_previous,
):
    slots, _, width = blocks.shape
    rank = item_factor.shape[1]
    rows_i, rows_t = item_factor.shape[0], time_factor.shape[0]
    range_tiles = U_DEV * n_item // BS
    per_shard = rows_i // BS
    shift = (rows_t * n_user // BS - 1).bit_length()
    user_local = user_blocks - lax.axis_index("user") * range_tiles
    item_local = item_blocks // per_shard // n_item * per_shard + item_blocks % per_shard
    at = jnp.arange(slots, dtype=jnp.int32)
    key = jnp.where(at < block_counts[0], (item_local << shift) + time_blocks, DEAD)
    size = -(-(slots + UNROLL) // LANE) * LANE
    pad = ((0, size - slots),)
    key = jnp.pad(key, pad, constant_values=DEAD)[None]
    value = jnp.pad(at * 16 + user_local + 1, pad)[None]
    vmem = pl.BlockSpec(memory_space=pltpu.VMEM)
    smem = pl.BlockSpec(memory_space=pltpu.SMEM)
    block_rows = 2 * (rows_i + rows_t)
    items, times, table = pl.pallas_call(
        functools.partial(gather_kernel, n_user),
        out_shape=(
            jax.ShapeDtypeStruct((2, rows_i * n_user, rank), jnp.bfloat16),
            jax.ShapeDtypeStruct((2, rows_t * n_user, rank), jnp.bfloat16),
            jax.ShapeDtypeStruct((8, size), jnp.int32),
        ),
        in_specs=[vmem] * 6,
        out_specs=(vmem, vmem, vmem),
        scratch_shapes=[
            pltpu.VMEM((block_rows, rank), jnp.bfloat16),
            pltpu.VMEM((n_user, block_rows, rank), jnp.bfloat16),
            pltpu.SemaphoreType.DMA((n_user,)),
            pltpu.SemaphoreType.DMA((n_user,)),
        ],
        compiler_params=pltpu.CompilerParams(
            collective_id=0, has_side_effects=True, vmem_limit_bytes=32 << 20
        ),
        name="gather",
    )(key, value, item_factor, item_previous, time_factor, time_previous)
    part = pl.pallas_call(
        functools.partial(product_kernel, shift),
        out_shape=jax.ShapeDtypeStruct((n_item, 2, U_DEV, rank), jnp.float32),
        in_specs=[smem, vmem, vmem, pl.BlockSpec(memory_space=pl.ANY)],
        out_specs=vmem,
        scratch_shapes=[
            pltpu.VMEM(blocks.shape, jnp.bfloat16),
            pltpu.VMEM((2, rows_i * n_user // BS, BS * BS, rank), jnp.bfloat16),
            pltpu.VMEM((2, range_tiles + 1, BS, rank), jnp.float32),
            pltpu.SemaphoreType.DMA,
        ],
        compiler_params=pltpu.CompilerParams(vmem_limit_bytes=48 << 20),
        name="products",
    )(table, items, times, blocks)
    return pl.pallas_call(
        finish_kernel,
        out_shape=(
            jax.ShapeDtypeStruct((2, U_DEV, rank), jnp.float32),
            jax.ShapeDtypeStruct((2, rank, rank), jnp.float32),
        ),
        in_specs=[vmem] * 3,
        out_specs=(vmem, vmem),
        scratch_shapes=[
            pltpu.VMEM((2, U_DEV, rank), jnp.float32),
            pltpu.VMEM((2, rows_i * n_user, rank), jnp.bfloat16),
            pltpu.SemaphoreType.DMA((2,)),
            pltpu.SemaphoreType.DMA((2,)),
        ],
        compiler_params=pltpu.CompilerParams(
            collective_id=1, has_side_effects=True, vmem_limit_bytes=32 << 20
        ),
        name="finish",
    )(part, items, times)


def solution(mesh):
    in_specs = (
        P(("groups", "user", "item"), None, None),
        P(("groups", "user", "item")),
        P(("groups", "user", "item")),
        P(("groups", "user", "item")),
        P(("groups", "user", "item")),
        P(("groups", "user", "item"), None),
        P(("groups", "user", "item"), None),
        P(("groups", "user"), None),
        P(("groups", "user"), None),
    )
    out_specs = (P(None, ("groups", "user", "item"), None), P("groups", None, None))
    body = functools.partial(local, mesh.shape["user"], mesh.shape["item"])
    return jax.shard_map(body, mesh=mesh, in_specs=in_specs, out_specs=out_specs, check_vma=False)
```

```python
import functools

import jax
import jax.numpy as jnp
from jax import lax
from jax.experimental import pallas as pl
from jax.experimental.pallas import tpu as pltpu
from jax.sharding import PartitionSpec as P

BS = 16
U_DEV = 64
LANE = 128
WIDTH = 4
UNROLL = 16
SHIFT = 13
PLANE = 4

extrapolation = 0.5


def extended(current, previous):
    wide_now = current.astype(jnp.float32)
    grown = wide_now + extrapolation * (wide_now - previous.astype(jnp.float32))
    return grown.astype(jnp.bfloat16)


def as_columns(row, size):
    parts = []
    for at in range(0, size, LANE):
        square = jnp.broadcast_to(row[:, at : at + LANE], (LANE, LANE))
        parts.append(square.T)
    return jnp.concatenate(parts, axis=0)


def order_slots(word, size):
    down = lax.broadcasted_iota(jnp.int32, (size, LANE), 0)
    across = lax.broadcasted_iota(jnp.int32, (1, LANE), 1)
    key = word >> SHIFT
    key_col = as_columns(key, size)
    places = []
    for at in range(0, size, LANE):
        earlier = (key_col == key[:, at : at + LANE]) & (down < across + at)
        places.append(jnp.sum(earlier.astype(jnp.int32), axis=0, keepdims=True))
    place = jnp.concatenate(places, axis=1)
    return jnp.where(word >= 0, key * size + place, jnp.int32(2**31 - 1)), place


def group_slots(word, order, place, size):
    order_col = as_columns(order, size)
    leads = (order_col & (WIDTH - 1)) == 0
    groups = []
    for at in range(0, size, LANE):
        ahead = leads & (order_col <= order[:, at : at + LANE])
        groups.append(jnp.sum(ahead.astype(jnp.int32), axis=0, keepdims=True))
    group = jnp.concatenate(groups, axis=1) - 1
    spot = jnp.where(word >= 0, group * WIDTH + (place & (WIDTH - 1)), -1)
    return spot, jnp.sum(leads.astype(jnp.int32), axis=0, keepdims=True)


def fill_table(word, spot, total, table_ref, size):
    across = lax.broadcasted_iota(jnp.int32, (1, LANE), 1)
    spot_col = as_columns(spot, size)
    word_col = as_columns(word, size)
    zero = jnp.zeros_like(word_col)
    table_ref[...] = jnp.zeros(table_ref.shape, jnp.int32)
    for at in range(0, size, LANE):
        for m in range(WIDTH):
            here = spot_col == (across + at) * WIDTH + m
            picked = jnp.sum(jnp.where(here, word_col, zero), axis=0, keepdims=True)
            table_ref[m : m + 1, at : at + LANE] = picked
    table_ref[WIDTH : WIDTH + 1, 0:LANE] = total


def flip(index, bits):
    bit = 1
    while bit <= bits:
        if bits & bit:
            index = index + bit - 2 * bit * ((index // bit) % 2)
        bit *= 2
    return index


def gather_kernel(
    n_user, plane, word_ref, item_hbm, item_old_hbm, time_hbm, time_old_hbm,
    items_ref, times_ref, table_ref, item_ref, item_old_ref, time_ref, time_old_ref, own, held, crossed,
    load_sem, line_send, plane_send, cross_send, recv, cross_recv,
):
    lines = n_user // plane
    me, core = lax.axis_index("user"), lax.axis_index("item")
    line, spot = me // plane, me % plane
    rows_i, rows_t = item_ref.shape[0], time_ref.shape[0]
    loads = [
        pltpu.make_async_copy(src, dst, load_sem.at[n])
        for n, (src, dst) in enumerate(
            ((item_hbm, item_ref), (item_old_hbm, item_old_ref), (time_hbm, time_ref), (time_old_hbm, time_old_ref))
        )
    ]
    for load in loads:
        load.start()
    barrier = pltpu.get_barrier_semaphore()

    def to(user):
        return {"user": user}

    line_peers = [flip(line, d) * plane + spot for d in range(1, lines)]
    plane_peers = [line * plane + flip(spot, d) for d in range(1, plane)]
    for peer in line_peers + plane_peers:
        pl.semaphore_signal(barrier, inc=1, device_id=to(peer), device_id_type=pl.DeviceIdType.MESH)
    pl.semaphore_signal(barrier, inc=1, device_id={"item": 1 - core}, device_id_type=pl.DeviceIdType.MESH)
    for load in loads:
        load.wait()
    item, time = item_ref[...], time_ref[...]
    item_new, time_new = extended(item, item_old_ref[...]), extended(time, time_old_ref[...])
    own[0:rows_i] = item
    own[rows_i : 2 * rows_i] = item_new
    first = jnp.broadcast_to(core, time.shape) == 0
    own[2 * rows_i :] = jnp.where(first, time.astype(jnp.float32), time_new.astype(jnp.float32)).astype(jnp.bfloat16)
    pl.semaphore_wait(barrier, lines + plane - 1)

    def copy(src, dst, send, receive, device):
        return pltpu.make_async_remote_copy(
            src_ref=src, dst_ref=dst, send_sem=send, recv_sem=receive,
            device_id=device, device_id_type=pl.DeviceIdType.MESH,
        )

    sends = []
    for d in range(1, lines):
        sends.append(copy(own, held.at[me], line_send.at[d], recv.at[me], to(line_peers[d - 1])))
    for d in range(1, plane):
        sends.append(copy(own, held.at[me], plane_send.at[0, d], recv.at[me], to(plane_peers[d - 1])))
    for send in sends:
        send.start()

    def arrive(source):
        copy(held.at[source], held.at[source], line_send.at[0], recv.at[source], to(source)).wait_recv()

    def across(source, n):
        return copy(
            held.at[source, pl.ds(2 * rows_i, rows_t)], crossed.at[source],
            cross_send.at[n], cross_recv.at[source], {"item": 1 - core},
        )

    def forward(d):
        source = line_peers[d - 1]
        arrive(source)
        for e in range(1, plane):
            sends.append(copy(held.at[source], held.at[source], plane_send.at[d, e], recv.at[source], to(plane_peers[e - 1])))
            sends[-1].start()
        sends.append(across(source, d * plane))
        sends[-1].start()

    size = word_ref.shape[1]
    word = word_ref[...]
    order, place = order_slots(word, size)
    if lines > 1:
        forward(1)
    slot, total = group_slots(word, order, place, size)
    for d in range(2, lines):
        forward(d)
    fill_table(word, slot, total, table_ref, size)

    def put(source, block):
        at_i = pl.multiple_of(source * rows_i, rows_i)
        at_t = pl.multiple_of(source * rows_t, rows_t)
        for s in range(2):
            items_ref[s, pl.ds(at_i, rows_i)] = block[s * rows_i : (s + 1) * rows_i]
        times_ref[core, pl.ds(at_t, rows_t)] = block[2 * rows_i :]

    at_me = pl.multiple_of(me * rows_t, rows_t)
    times_ref[0, pl.ds(at_me, rows_t)] = time
    times_ref[1, pl.ds(at_me, rows_t)] = time_new
    for s, rows in enumerate((item, item_new)):
        items_ref[s, pl.ds(pl.multiple_of(me * rows_i, rows_i), rows_i)] = rows
    sources = [(d * plane, line_peers[d - 1]) for d in range(1, lines)]
    for d in range(lines):
        for e in range(1, plane):
            source = flip(line, d) * plane + flip(spot, e)
            arrive(source)
            sends.append(across(source, d * plane + e))
            sends[-1].start()
            sources.append((d * plane + e, source))
    for n, source in sources:
        put(source, held.at[source])
    for n, source in sources:
        across(source, n).wait_recv()
        at_t = pl.multiple_of(source * rows_t, rows_t)
        times_ref[1 - core, pl.ds(at_t, rows_t)] = crossed[source]
    for send in sends:
        send.wait_send()


def product_kernel(
    shift, table_hbm, items_ref, times_ref, blocks_ref, part_ref, tensor, spread, acc, table_ref, sem, table_sem
):
    rank = items_ref.shape[2]
    load = pltpu.make_async_copy(blocks_ref, tensor, sem)
    load.start()
    plan = pltpu.make_async_copy(table_hbm, table_ref, table_sem)
    plan.start()
    acc[...] = jnp.zeros_like(acc)

    def widen(tile, carry):
        at = pl.multiple_of(tile * BS, BS)
        for s in range(2):
            rows = items_ref[s, pl.ds(at, BS)].astype(jnp.float32)
            for j in range(BS):
                wide = jnp.broadcast_to(rows[j : j + 1], (BS, rank))
                spread[s, tile, j * BS : (j + 1) * BS] = wide.astype(jnp.bfloat16)
        return carry

    lax.fori_loop(0, items_ref.shape[1] // BS, widen, 0)
    plan.wait()
    load.wait()
    count = table_ref[WIDTH, 0]

    def turn(g, carry):
        for v in range(UNROLL):
            c = g * UNROLL + v
            member = [table_ref[m, c] for m in range(WIDTH)]
            key = member[0] >> SHIFT
            tile = key >> shift
            at = pl.multiple_of((key & ((1 << shift) - 1)) * BS, BS)
            x = jnp.concatenate([tensor[(word >> 4) & 511] for word in member], axis=0)
            for s in range(2):
                right = times_ref[s, pl.ds(at, BS)]
                left = spread[s, tile].reshape(BS, BS, rank)
                khatri = (left * right[None]).reshape(BS * BS, rank)
                y = jnp.dot(x, khatri, preferred_element_type=jnp.float32)
                for m, word in enumerate(member):
                    acc[s, word & 15] += y[m * BS : (m + 1) * BS]
        return carry

    lax.fori_loop(0, (count + UNROLL - 1) // UNROLL, turn, 0)
    tiles = U_DEV // BS
    for half in range(part_ref.shape[0]):
        for s in range(2):
            for n in range(tiles):
                part_ref[half, s, n * BS : (n + 1) * BS] = acc[s, 1 + half * tiles + n]


def gram(rows):
    return lax.dot_general(rows, rows, (((0,), (0,)), ((), ())), preferred_element_type=jnp.float32)


def finish_kernel(part_ref, items_ref, times_ref, rows_ref, grams_ref, theirs, items, send_sem, recv_sem):
    me = lax.axis_index("item")
    other = 1 - me
    barrier = pltpu.get_barrier_semaphore()
    pl.semaphore_signal(barrier, inc=1, device_id={"item": other}, device_id_type=pl.DeviceIdType.MESH)
    pl.semaphore_wait(barrier, 1)
    copies = []
    for n, (src, dst) in enumerate(((part_ref.at[other], theirs), (items_ref, items))):
        copies.append(
            pltpu.make_async_remote_copy(
                src_ref=src, dst_ref=dst, send_sem=send_sem.at[n], recv_sem=recv_sem.at[n],
                device_id={"item": other}, device_id_type=pl.DeviceIdType.MESH,
            )
        )
        copies[-1].start()
    mine = [gram(items_ref[s]) for s in range(2)]
    times = [gram(times_ref[s]) for s in range(2)]
    copies[0].wait()
    rows_ref[...] = part_ref[me] + theirs[...]
    copies[1].wait()
    for s in range(2):
        grams_ref[s] = (mine[s] + gram(items[s])) * times[s]


def local(
    n_user, n_item, blocks, user_blocks, item_blocks, time_blocks, block_counts,
    item_factor, item_previous, time_factor, time_previous,
):
    slots, _, width = blocks.shape
    rank = item_factor.shape[1]
    rows_i, rows_t = item_factor.shape[0], time_factor.shape[0]
    range_tiles = U_DEV * n_item // BS
    per_shard = rows_i // BS
    shift = (rows_t * n_user // BS - 1).bit_length()
    user_local = user_blocks - lax.axis_index("user") * range_tiles
    item_local = item_blocks // per_shard // n_item * per_shard + item_blocks % per_shard
    at = jnp.arange(slots, dtype=jnp.int32)
    word = (((item_local << shift) + time_blocks) << SHIFT) + at * 16 + user_local + 1
    word = jnp.where(at < block_counts[0], word, -1)
    size = -(-(slots + UNROLL) // LANE) * LANE
    word = jnp.pad(word, ((0, size - slots),), constant_values=-1)[None]
    vmem = pl.BlockSpec(memory_space=pltpu.VMEM)
    hbm = pl.BlockSpec(memory_space=pl.ANY)
    plane = PLANE if n_user % PLANE == 0 else 1
    block_rows = 2 * rows_i + rows_t
    dma = pltpu.SemaphoreType.DMA
    items, times, table = pl.pallas_call(
        functools.partial(gather_kernel, n_user, plane),
        out_shape=(
            jax.ShapeDtypeStruct((2, rows_i * n_user, rank), jnp.bfloat16),
            jax.ShapeDtypeStruct((2, rows_t * n_user, rank), jnp.bfloat16),
            jax.ShapeDtypeStruct((8, size), jnp.int32),
        ),
        in_specs=[vmem] + [hbm] * 4,
        out_specs=(vmem, vmem, vmem),
        scratch_shapes=[
            pltpu.VMEM((rows_i, rank), jnp.bfloat16),
            pltpu.VMEM((rows_i, rank), jnp.bfloat16),
            pltpu.VMEM((rows_t, rank), jnp.bfloat16),
            pltpu.VMEM((rows_t, rank), jnp.bfloat16),
            pltpu.VMEM((block_rows, rank), jnp.bfloat16),
            pltpu.VMEM((n_user, block_rows, rank), jnp.bfloat16),
            pltpu.VMEM((n_user, rows_t, rank), jnp.bfloat16),
            dma((4,)),
            dma((n_user // plane,)),
            dma((n_user // plane, plane)),
            dma((n_user,)),
            dma((n_user,)),
            dma((n_user,)),
        ],
        compiler_params=pltpu.CompilerParams(
            collective_id=0, has_side_effects=True, vmem_limit_bytes=32 << 20
        ),
        name="gather",
    )(word, item_factor, item_previous, time_factor, time_previous)
    part = pl.pallas_call(
        functools.partial(product_kernel, shift),
        out_shape=jax.ShapeDtypeStruct((n_item, 2, U_DEV, rank), jnp.float32),
        in_specs=[hbm, vmem, vmem, hbm],
        out_specs=vmem,
        scratch_shapes=[
            pltpu.VMEM(blocks.shape, jnp.bfloat16),
            pltpu.VMEM((2, rows_i * n_user // BS, BS * BS, rank), jnp.bfloat16),
            pltpu.VMEM((2, range_tiles + 1, BS, rank), jnp.float32),
            pltpu.SMEM((8, size), jnp.int32),
            dma,
            dma,
        ],
        compiler_params=pltpu.CompilerParams(vmem_limit_bytes=48 << 20),
        name="products",
    )(table, items, times, blocks)
    return pl.pallas_call(
        finish_kernel,
        out_shape=(
            jax.ShapeDtypeStruct((2, U_DEV, rank), jnp.float32),
            jax.ShapeDtypeStruct((2, rank, rank), jnp.float32),
        ),
        in_specs=[vmem] * 3,
        out_specs=(vmem, vmem),
        scratch_shapes=[
            pltpu.VMEM((2, U_DEV, rank), jnp.float32),
            pltpu.VMEM((2, rows_i * n_user, rank), jnp.bfloat16),
            pltpu.SemaphoreType.DMA((2,)),
            pltpu.SemaphoreType.DMA((2,)),
        ],
        compiler_params=pltpu.CompilerParams(
            collective_id=1, has_side_effects=True, vmem_limit_bytes=32 << 20
        ),
        name="finish",
    )(part, items, times)


def solution(mesh):
    in_specs = (
        P(("groups", "user", "item"), None, None),
        P(("groups", "user", "item")),
        P(("groups", "user", "item")),
        P(("groups", "user", "item")),
        P(("groups", "user", "item")),
        P(("groups", "user", "item"), None),
        P(("groups", "user", "item"), None),
        P(("groups", "user"), None),
        P(("groups", "user"), None),
    )
    out_specs = (P(None, ("groups", "user", "item"), None), P("groups", None, None))
    body = functools.partial(local, mesh.shape["user"], mesh.shape["item"])
    return jax.shard_map(body, mesh=mesh, in_specs=in_specs, out_specs=out_specs, check_vma=False)
```

```python
import functools

import jax
import jax.numpy as jnp
from jax import lax
from jax.experimental import pallas as pl
from jax.experimental.pallas import tpu as pltpu
from jax.sharding import PartitionSpec as P

BS = 16
U_DEV = 64
LANE = 128
WIDTH = 4
UNROLL = 16
SHIFT = 13
PLANE = 4

extrapolation = 0.5


def extended(current, previous):
    wide_now = current.astype(jnp.float32)
    grown = wide_now + extrapolation * (wide_now - previous.astype(jnp.float32))
    return grown.astype(jnp.bfloat16)


def as_columns(row, size):
    parts = []
    for at in range(0, size, LANE):
        square = jnp.broadcast_to(row[:, at : at + LANE], (LANE, LANE))
        parts.append(square.T)
    return jnp.concatenate(parts, axis=0)


def order_slots(word, size):
    down = lax.broadcasted_iota(jnp.int32, (size, LANE), 0)
    across = lax.broadcasted_iota(jnp.int32, (1, LANE), 1)
    key = word >> SHIFT
    key_col = as_columns(key, size)
    places = []
    for at in range(0, size, LANE):
        earlier = (key_col == key[:, at : at + LANE]) & (down < across + at)
        places.append(jnp.sum(earlier.astype(jnp.int32), axis=0, keepdims=True))
    place = jnp.concatenate(places, axis=1)
    return jnp.where(word >= 0, key * size + place, jnp.int32(2**31 - 1)), place


def group_slots(word, order, place, size):
    order_col = as_columns(order, size)
    leads = (order_col & (WIDTH - 1)) == 0
    groups = []
    for at in range(0, size, LANE):
        ahead = leads & (order_col <= order[:, at : at + LANE])
        groups.append(jnp.sum(ahead.astype(jnp.int32), axis=0, keepdims=True))
    group = jnp.concatenate(groups, axis=1) - 1
    spot = jnp.where(word >= 0, group * WIDTH + (place & (WIDTH - 1)), -1)
    return spot, jnp.sum(leads.astype(jnp.int32), axis=0, keepdims=True)


def fill_table(word, spot, total, table_ref, size):
    across = lax.broadcasted_iota(jnp.int32, (1, LANE), 1)
    spot_col = as_columns(spot, size)
    word_col = as_columns(word, size)
    zero = jnp.zeros_like(word_col)
    table_ref[...] = jnp.zeros(table_ref.shape, jnp.int32)
    for at in range(0, size, LANE):
        for m in range(WIDTH):
            here = spot_col == (across + at) * WIDTH + m
            picked = jnp.sum(jnp.where(here, word_col, zero), axis=0, keepdims=True)
            table_ref[m : m + 1, at : at + LANE] = picked
    table_ref[WIDTH : WIDTH + 1, 0:LANE] = total


def flip(index, bits):
    bit = 1
    while bit <= bits:
        if bits & bit:
            index = index + bit - 2 * bit * ((index // bit) % 2)
        bit *= 2
    return index


def gather_kernel(
    n_user, plane, word_ref, item_hbm, item_old_hbm, time_hbm, time_old_hbm,
    items_ref, times_ref, table_ref, item_ref, item_old_ref, time_ref, time_old_ref, own, held, crossed,
    load_sem, line_send, plane_send, cross_send, recv, cross_recv,
):
    lines = n_user // plane
    me, core = lax.axis_index("user"), lax.axis_index("item")
    line, spot = me // plane, me % plane
    rows_i, rows_t = item_ref.shape[0], time_ref.shape[0]
    loads = [
        pltpu.make_async_copy(src, dst, load_sem.at[n])
        for n, (src, dst) in enumerate(
            ((item_hbm, item_ref), (item_old_hbm, item_old_ref), (time_hbm, time_ref), (time_old_hbm, time_old_ref))
        )
    ]
    for load in loads:
        load.start()
    barrier = pltpu.get_barrier_semaphore()

    def to(user):
        return {"user": user}

    line_peers = [flip(line, d) * plane + spot for d in range(1, lines)]
    plane_peers = [line * plane + flip(spot, d) for d in range(1, plane)]
    for peer in line_peers + plane_peers:
        pl.semaphore_signal(barrier, inc=1, device_id=to(peer), device_id_type=pl.DeviceIdType.MESH)
    pl.semaphore_signal(barrier, inc=1, device_id={"item": 1 - core}, device_id_type=pl.DeviceIdType.MESH)
    for load in loads:
        load.wait()
    item, time = item_ref[...], time_ref[...]
    item_new, time_new = extended(item, item_old_ref[...]), extended(time, time_old_ref[...])
    own[0:rows_i] = item
    own[rows_i : 2 * rows_i] = item_new
    first = jnp.broadcast_to(core, time.shape) == 0
    own[2 * rows_i :] = jnp.where(first, time.astype(jnp.float32), time_new.astype(jnp.float32)).astype(jnp.bfloat16)
    pl.semaphore_wait(barrier, lines + plane - 1)

    def copy(src, dst, send, receive, device):
        return pltpu.make_async_remote_copy(
            src_ref=src, dst_ref=dst, send_sem=send, recv_sem=receive,
            device_id=device, device_id_type=pl.DeviceIdType.MESH,
        )

    sends = []
    for d in range(1, lines):
        sends.append(copy(own, held.at[me], line_send.at[d], recv.at[me], to(line_peers[d - 1])))
    for d in range(1, plane):
        sends.append(copy(own, held.at[me], plane_send.at[0, d], recv.at[me], to(plane_peers[d - 1])))
    for send in sends:
        send.start()

    def arrive(source):
        copy(held.at[source], held.at[source], line_send.at[0], recv.at[source], to(source)).wait_recv()

    def across(source, n):
        return copy(
            held.at[source, pl.ds(2 * rows_i, rows_t)], crossed.at[source],
            cross_send.at[n], cross_recv.at[source], {"item": 1 - core},
        )

    def forward(d):
        source = line_peers[d - 1]
        arrive(source)
        for e in range(1, plane):
            sends.append(copy(held.at[source], held.at[source], plane_send.at[d, e], recv.at[source], to(plane_peers[e - 1])))
            sends[-1].start()
        sends.append(across(source, d * plane))
        sends[-1].start()

    size = word_ref.shape[1]
    word = word_ref[...]
    order, place = order_slots(word, size)
    if lines > 1:
        forward(1)
    slot, total = group_slots(word, order, place, size)
    for d in range(2, lines):
        forward(d)
    fill_table(word, slot, total, table_ref, size)

    def put(source, block):
        at_i = pl.multiple_of(source * rows_i, rows_i)
        at_t = pl.multiple_of(source * rows_t, rows_t)
        for s in range(2):
            items_ref[s, pl.ds(at_i, rows_i)] = block[s * rows_i : (s + 1) * rows_i]
        times_ref[core, pl.ds(at_t, rows_t)] = block[2 * rows_i :]

    at_me = pl.multiple_of(me * rows_t, rows_t)
    times_ref[0, pl.ds(at_me, rows_t)] = time
    times_ref[1, pl.ds(at_me, rows_t)] = time_new
    for s, rows in enumerate((item, item_new)):
        items_ref[s, pl.ds(pl.multiple_of(me * rows_i, rows_i), rows_i)] = rows
    sources = [(d * plane, line_peers[d - 1]) for d in range(1, lines)]
    for d in range(lines):
        for e in range(1, plane):
            source = flip(line, d) * plane + flip(spot, e)
            arrive(source)
            sends.append(across(source, d * plane + e))
            sends[-1].start()
            sources.append((d * plane + e, source))
    for n, source in sources:
        put(source, held.at[source])
    for n, source in sources:
        across(source, n).wait_recv()
        at_t = pl.multiple_of(source * rows_t, rows_t)
        times_ref[1 - core, pl.ds(at_t, rows_t)] = crossed[source]
    for send in sends:
        send.wait_send()


def product_kernel(
    shift, table_hbm, items_ref, times_ref, blocks_ref, part_ref, tensor, spread, table_ref, sem, table_sem, *totals
):
    rank = items_ref.shape[2]
    load = pltpu.make_async_copy(blocks_ref, tensor, sem)
    load.start()
    plan = pltpu.make_async_copy(table_hbm, table_ref, table_sem)
    plan.start()
    for total in totals:
        total[...] = jnp.zeros_like(total)

    def widen(tile, carry):
        at = pl.multiple_of(tile * BS, BS)
        for s in range(2):
            rows = items_ref[s, pl.ds(at, BS)].astype(jnp.float32)
            for j in range(BS):
                wide = jnp.broadcast_to(rows[j : j + 1], (BS, rank))
                spread[s, tile, j * BS : (j + 1) * BS] = wide.astype(jnp.bfloat16)
        return carry

    lax.fori_loop(0, items_ref.shape[1] // BS, widen, 0)
    plan.wait()
    load.wait()
    count = table_ref[WIDTH, 0]

    def turn(g, carry):
        for v in range(UNROLL):
            c = g * UNROLL + v
            member = [table_ref[m, c] for m in range(WIDTH)]
            key = member[0] >> SHIFT
            tile = key >> shift
            at = pl.multiple_of((key & ((1 << shift) - 1)) * BS, BS)
            x = jnp.concatenate([tensor[(word >> 4) & 511] for word in member], axis=0)
            for s in range(2):
                right = times_ref[s, pl.ds(at, BS)]
                left = spread[s, tile].reshape(BS, BS, rank)
                khatri = (left * right[None]).reshape(BS * BS, rank)
                y = jnp.dot(x, khatri, preferred_element_type=jnp.float32)
                for m, word in enumerate(member):
                    totals[m * 2 + s][word & 15] += y[m * BS : (m + 1) * BS]
        return carry

    lax.fori_loop(0, (count + UNROLL - 1) // UNROLL, turn, 0)
    tiles = U_DEV // BS
    for half in range(part_ref.shape[0]):
        for s in range(2):
            for n in range(tiles):
                part_ref[half, s, n * BS : (n + 1) * BS] = sum(
                    totals[m * 2 + s][1 + half * tiles + n] for m in range(WIDTH)
                )


def gram(rows):
    return lax.dot_general(rows, rows, (((0,), (0,)), ((), ())), preferred_element_type=jnp.float32)


def finish_kernel(part_ref, items_ref, times_ref, rows_ref, grams_ref, theirs, items, send_sem, recv_sem):
    me = lax.axis_index("item")
    other = 1 - me
    barrier = pltpu.get_barrier_semaphore()
    pl.semaphore_signal(barrier, inc=1, device_id={"item": other}, device_id_type=pl.DeviceIdType.MESH)
    pl.semaphore_wait(barrier, 1)
    copies = []
    for n, (src, dst) in enumerate(((part_ref.at[other], theirs), (items_ref, items))):
        copies.append(
            pltpu.make_async_remote_copy(
                src_ref=src, dst_ref=dst, send_sem=send_sem.at[n], recv_sem=recv_sem.at[n],
                device_id={"item": other}, device_id_type=pl.DeviceIdType.MESH,
            )
        )
        copies[-1].start()
    mine = [gram(items_ref[s]) for s in range(2)]
    times = [gram(times_ref[s]) for s in range(2)]
    copies[0].wait()
    rows_ref[...] = part_ref[me] + theirs[...]
    copies[1].wait()
    for s in range(2):
        grams_ref[s] = (mine[s] + gram(items[s])) * times[s]


def local(
    n_user, n_item, blocks, user_blocks, item_blocks, time_blocks, block_counts,
    item_factor, item_previous, time_factor, time_previous,
):
    slots, _, width = blocks.shape
    rank = item_factor.shape[1]
    rows_i, rows_t = item_factor.shape[0], time_factor.shape[0]
    range_tiles = U_DEV * n_item // BS
    per_shard = rows_i // BS
    shift = (rows_t * n_user // BS - 1).bit_length()
    user_local = user_blocks - lax.axis_index("user") * range_tiles
    item_local = item_blocks // per_shard // n_item * per_shard + item_blocks % per_shard
    at = jnp.arange(slots, dtype=jnp.int32)
    word = (((item_local << shift) + time_blocks) << SHIFT) + at * 16 + user_local + 1
    word = jnp.where(at < block_counts[0], word, -1)
    size = -(-(slots + UNROLL) // LANE) * LANE
    word = jnp.pad(word, ((0, size - slots),), constant_values=-1)[None]
    vmem = pl.BlockSpec(memory_space=pltpu.VMEM)
    hbm = pl.BlockSpec(memory_space=pl.ANY)
    plane = PLANE if n_user % PLANE == 0 else 1
    block_rows = 2 * rows_i + rows_t
    dma = pltpu.SemaphoreType.DMA
    items, times, table = pl.pallas_call(
        functools.partial(gather_kernel, n_user, plane),
        out_shape=(
            jax.ShapeDtypeStruct((2, rows_i * n_user, rank), jnp.bfloat16),
            jax.ShapeDtypeStruct((2, rows_t * n_user, rank), jnp.bfloat16),
            jax.ShapeDtypeStruct((8, size), jnp.int32),
        ),
        in_specs=[vmem] + [hbm] * 4,
        out_specs=(vmem, vmem, vmem),
        scratch_shapes=[
            pltpu.VMEM((rows_i, rank), jnp.bfloat16),
            pltpu.VMEM((rows_i, rank), jnp.bfloat16),
            pltpu.VMEM((rows_t, rank), jnp.bfloat16),
            pltpu.VMEM((rows_t, rank), jnp.bfloat16),
            pltpu.VMEM((block_rows, rank), jnp.bfloat16),
            pltpu.VMEM((n_user, block_rows, rank), jnp.bfloat16),
            pltpu.VMEM((n_user, rows_t, rank), jnp.bfloat16),
            dma((4,)),
            dma((n_user // plane,)),
            dma((n_user // plane, plane)),
            dma((n_user,)),
            dma((n_user,)),
            dma((n_user,)),
        ],
        compiler_params=pltpu.CompilerParams(
            collective_id=0, has_side_effects=True, vmem_limit_bytes=60 << 20
        ),
        name="gather",
    )(word, item_factor, item_previous, time_factor, time_previous)
    part = pl.pallas_call(
        functools.partial(product_kernel, shift),
        out_shape=jax.ShapeDtypeStruct((n_item, 2, U_DEV, rank), jnp.float32),
        in_specs=[hbm, vmem, vmem, hbm],
        out_specs=vmem,
        scratch_shapes=[
            pltpu.VMEM(blocks.shape, jnp.bfloat16),
            pltpu.VMEM((2, rows_i * n_user // BS, BS * BS, rank), jnp.bfloat16),
            pltpu.SMEM((8, size), jnp.int32),
            dma,
            dma,
        ]
        + [pltpu.VMEM((range_tiles + 1, BS, rank), jnp.float32)] * (2 * WIDTH),
        compiler_params=pltpu.CompilerParams(vmem_limit_bytes=60 << 20),
        name="products",
    )(table, items, times, blocks)
    return pl.pallas_call(
        finish_kernel,
        out_shape=(
            jax.ShapeDtypeStruct((2, U_DEV, rank), jnp.float32),
            jax.ShapeDtypeStruct((2, rank, rank), jnp.float32),
        ),
        in_specs=[vmem] * 3,
        out_specs=(vmem, vmem),
        scratch_shapes=[
            pltpu.VMEM((2, U_DEV, rank), jnp.float32),
            pltpu.VMEM((2, rows_i * n_user, rank), jnp.bfloat16),
            pltpu.SemaphoreType.DMA((2,)),
            pltpu.SemaphoreType.DMA((2,)),
        ],
        compiler_params=pltpu.CompilerParams(
            collective_id=1, has_side_effects=True, vmem_limit_bytes=32 << 20
        ),
        name="finish",
    )(part, items, times)


def solution(mesh):
    in_specs = (
        P(("groups", "user", "item"), None, None),
        P(("groups", "user", "item")),
        P(("groups", "user", "item")),
        P(("groups", "user", "item")),
        P(("groups", "user", "item")),
        P(("groups", "user", "item"), None),
        P(("groups", "user", "item"), None),
        P(("groups", "user"), None),
        P(("groups", "user"), None),
    )
    out_specs = (P(None, ("groups", "user", "item"), None), P("groups", None, None))
    body = functools.partial(local, mesh.shape["user"], mesh.shape["item"])
    return jax.shard_map(body, mesh=mesh, in_specs=in_specs, out_specs=out_specs, check_vma=False)
```

```python
import functools

import jax
import jax.numpy as jnp
from jax import lax
from jax.experimental import pallas as pl
from jax.experimental.pallas import tpu as pltpu
from jax.sharding import PartitionSpec as P

BS = 16
U_DEV = 64
LANE = 128
WIDTH = 4
UNROLL = 16
SHIFT = 13
PLANE = 4

extrapolation = 0.5


def extended(current, previous):
    wide_now = current.astype(jnp.float32)
    grown = wide_now + extrapolation * (wide_now - previous.astype(jnp.float32))
    return grown.astype(jnp.bfloat16)


def as_columns(row, size):
    parts = []
    for at in range(0, size, LANE):
        square = jnp.broadcast_to(row[:, at : at + LANE], (LANE, LANE))
        parts.append(square.T)
    return jnp.concatenate(parts, axis=0)


def order_slots(word, size):
    down = lax.broadcasted_iota(jnp.int32, (size, LANE), 0)
    across = lax.broadcasted_iota(jnp.int32, (1, LANE), 1)
    key = word >> SHIFT
    key_col = as_columns(key, size)
    places = []
    for at in range(0, size, LANE):
        earlier = (key_col == key[:, at : at + LANE]) & (down < across + at)
        places.append(jnp.sum(earlier.astype(jnp.int32), axis=0, keepdims=True))
    place = jnp.concatenate(places, axis=1)
    return jnp.where(word >= 0, key * size + place, jnp.int32(2**31 - 1)), place


def group_slots(word, order, place, size):
    order_col = as_columns(order, size)
    leads = (order_col & (WIDTH - 1)) == 0
    groups = []
    for at in range(0, size, LANE):
        ahead = leads & (order_col <= order[:, at : at + LANE])
        groups.append(jnp.sum(ahead.astype(jnp.int32), axis=0, keepdims=True))
    group = jnp.concatenate(groups, axis=1) - 1
    spot = jnp.where(word >= 0, group * WIDTH + (place & (WIDTH - 1)), -1)
    return spot, jnp.sum(leads.astype(jnp.int32), axis=0, keepdims=True)


def fill_table(word, spot, total, table_ref, size):
    across = lax.broadcasted_iota(jnp.int32, (1, LANE), 1)
    spot_col = as_columns(spot, size)
    word_col = as_columns(word, size)
    zero = jnp.zeros_like(word_col)
    table_ref[...] = jnp.zeros(table_ref.shape, jnp.int32)
    for at in range(0, size, LANE):
        for m in range(WIDTH):
            here = spot_col == (across + at) * WIDTH + m
            picked = jnp.sum(jnp.where(here, word_col, zero), axis=0, keepdims=True)
            table_ref[m : m + 1, at : at + LANE] = picked
    table_ref[WIDTH : WIDTH + 1, 0:LANE] = total


def flip(index, bits):
    bit = 1
    while bit <= bits:
        if bits & bit:
            index = index + bit - 2 * bit * ((index // bit) % 2)
        bit *= 2
    return index


def gather_kernel(
    n_user, plane, rows_i, word_ref, factors_ref,
    items_ref, times_ref, table_ref, own, held, crossed, line_send, plane_send, cross_send, recv, cross_recv,
):
    lines = n_user // plane
    me, core = lax.axis_index("user"), lax.axis_index("item")
    line, spot = me // plane, me % plane
    rows_t = factors_ref.shape[0] // 2 - rows_i
    barrier = pltpu.get_barrier_semaphore()

    def to(user):
        return {"user": user}

    line_peers = [flip(line, d) * plane + spot for d in range(1, lines)]
    plane_peers = [line * plane + flip(spot, d) for d in range(1, plane)]
    for peer in line_peers + plane_peers:
        pl.semaphore_signal(barrier, inc=1, device_id=to(peer), device_id_type=pl.DeviceIdType.MESH)
    pl.semaphore_signal(barrier, inc=1, device_id={"item": 1 - core}, device_id_type=pl.DeviceIdType.MESH)
    item, time = factors_ref[0:rows_i], factors_ref[2 * rows_i : 2 * rows_i + rows_t]
    item_new = extended(item, factors_ref[rows_i : 2 * rows_i])
    time_new = extended(time, factors_ref[2 * rows_i + rows_t :])
    own[0:rows_i] = item
    own[rows_i : 2 * rows_i] = item_new
    first = jnp.broadcast_to(core, time.shape) == 0
    own[2 * rows_i :] = jnp.where(first, time.astype(jnp.float32), time_new.astype(jnp.float32)).astype(jnp.bfloat16)
    pl.semaphore_wait(barrier, lines + plane - 1)

    def copy(src, dst, send, receive, device):
        return pltpu.make_async_remote_copy(
            src_ref=src, dst_ref=dst, send_sem=send, recv_sem=receive,
            device_id=device, device_id_type=pl.DeviceIdType.MESH,
        )

    sends = []
    for d in range(1, lines):
        sends.append(copy(own, held.at[me], line_send.at[d], recv.at[me], to(line_peers[d - 1])))
    for d in range(1, plane):
        sends.append(copy(own, held.at[me], plane_send.at[0, d], recv.at[me], to(plane_peers[d - 1])))
    for send in sends:
        send.start()

    def arrive(source):
        copy(held.at[source], held.at[source], line_send.at[0], recv.at[source], to(source)).wait_recv()

    def across(source, n):
        return copy(
            held.at[source, pl.ds(2 * rows_i, rows_t)], crossed.at[source],
            cross_send.at[n], cross_recv.at[source], {"item": 1 - core},
        )

    def forward(d):
        source = line_peers[d - 1]
        arrive(source)
        for e in range(1, plane):
            sends.append(copy(held.at[source], held.at[source], plane_send.at[d, e], recv.at[source], to(plane_peers[e - 1])))
            sends[-1].start()
        sends.append(across(source, d * plane))
        sends[-1].start()

    size = word_ref.shape[1]
    word = word_ref[...]
    order, place = order_slots(word, size)
    if lines > 1:
        forward(1)
    slot, total = group_slots(word, order, place, size)
    for d in range(2, lines):
        forward(d)
    fill_table(word, slot, total, table_ref, size)

    def put(source, block):
        at_i = pl.multiple_of(source * rows_i, rows_i)
        at_t = pl.multiple_of(source * rows_t, rows_t)
        for s in range(2):
            items_ref[s, pl.ds(at_i, rows_i)] = block[s * rows_i : (s + 1) * rows_i]
        times_ref[core, pl.ds(at_t, rows_t)] = block[2 * rows_i :]

    at_me = pl.multiple_of(me * rows_t, rows_t)
    times_ref[0, pl.ds(at_me, rows_t)] = time
    times_ref[1, pl.ds(at_me, rows_t)] = time_new
    for s, rows in enumerate((item, item_new)):
        items_ref[s, pl.ds(pl.multiple_of(me * rows_i, rows_i), rows_i)] = rows
    sources = [(d * plane, line_peers[d - 1]) for d in range(1, lines)]
    for d in range(lines):
        for e in range(1, plane):
            source = flip(line, d) * plane + flip(spot, e)
            arrive(source)
            sends.append(across(source, d * plane + e))
            sends[-1].start()
            sources.append((d * plane + e, source))
    for n, source in sources:
        put(source, held.at[source])
    for n, source in sources:
        across(source, n).wait_recv()
        at_t = pl.multiple_of(source * rows_t, rows_t)
        times_ref[1 - core, pl.ds(at_t, rows_t)] = crossed[source]
    for send in sends:
        send.wait_send()


def product_kernel(
    shift, table_hbm, items_ref, times_ref, tensor, part_ref, spread, table_ref, table_sem, *totals
):
    rank = items_ref.shape[2]
    plan = pltpu.make_async_copy(table_hbm, table_ref, table_sem)
    plan.start()
    for total in totals:
        total[...] = jnp.zeros_like(total)

    def widen(tile, carry):
        at = pl.multiple_of(tile * BS, BS)
        for s in range(2):
            rows = items_ref[s, pl.ds(at, BS)].astype(jnp.float32)
            for j in range(BS):
                wide = jnp.broadcast_to(rows[j : j + 1], (BS, rank))
                spread[s, tile, j * BS : (j + 1) * BS] = wide.astype(jnp.bfloat16)
        return carry

    lax.fori_loop(0, items_ref.shape[1] // BS, widen, 0)
    plan.wait()
    count = table_ref[WIDTH, 0]

    def turn(g, carry):
        for v in range(UNROLL):
            c = g * UNROLL + v
            member = [table_ref[m, c] for m in range(WIDTH)]
            key = member[0] >> SHIFT
            tile = key >> shift
            at = pl.multiple_of((key & ((1 << shift) - 1)) * BS, BS)
            x = jnp.concatenate([tensor[(word >> 4) & 511] for word in member], axis=0)
            for s in range(2):
                right = times_ref[s, pl.ds(at, BS)]
                left = spread[s, tile].reshape(BS, BS, rank)
                khatri = (left * right[None]).reshape(BS * BS, rank)
                y = jnp.dot(x, khatri, preferred_element_type=jnp.float32)
                for m, word in enumerate(member):
                    totals[m * 2 + s][word & 15] += y[m * BS : (m + 1) * BS]
        return carry

    lax.fori_loop(0, (count + UNROLL - 1) // UNROLL, turn, 0)
    tiles = U_DEV // BS
    for half in range(part_ref.shape[0]):
        for s in range(2):
            for n in range(tiles):
                part_ref[half, s, n * BS : (n + 1) * BS] = sum(
                    totals[m * 2 + s][1 + half * tiles + n] for m in range(WIDTH)
                )


def gram(rows):
    return lax.dot_general(rows, rows, (((0,), (0,)), ((), ())), preferred_element_type=jnp.float32)


def finish_kernel(part_ref, items_ref, times_ref, rows_ref, grams_ref, theirs, items, send_sem, recv_sem):
    me = lax.axis_index("item")
    other = 1 - me
    barrier = pltpu.get_barrier_semaphore()
    pl.semaphore_signal(barrier, inc=1, device_id={"item": other}, device_id_type=pl.DeviceIdType.MESH)
    pl.semaphore_wait(barrier, 1)
    copies = []
    for n, (src, dst) in enumerate(((part_ref.at[other], theirs), (items_ref, items))):
        copies.append(
            pltpu.make_async_remote_copy(
                src_ref=src, dst_ref=dst, send_sem=send_sem.at[n], recv_sem=recv_sem.at[n],
                device_id={"item": other}, device_id_type=pl.DeviceIdType.MESH,
            )
        )
        copies[-1].start()
    mine = [gram(items_ref[s]) for s in range(2)]
    times = [gram(times_ref[s]) for s in range(2)]
    copies[0].wait()
    rows_ref[...] = part_ref[me] + theirs[...]
    copies[1].wait()
    for s in range(2):
        grams_ref[s] = (mine[s] + gram(items[s])) * times[s]


def local(
    n_user, n_item, blocks, user_blocks, item_blocks, time_blocks, block_counts,
    item_factor, item_previous, time_factor, time_previous,
):
    slots, _, width = blocks.shape
    rank = item_factor.shape[1]
    rows_i, rows_t = item_factor.shape[0], time_factor.shape[0]
    range_tiles = U_DEV * n_item // BS
    per_shard = rows_i // BS
    shift = (rows_t * n_user // BS - 1).bit_length()
    user_local = user_blocks - lax.axis_index("user") * range_tiles
    item_local = item_blocks // per_shard // n_item * per_shard + item_blocks % per_shard
    at = jnp.arange(slots, dtype=jnp.int32)
    word = (((item_local << shift) + time_blocks) << SHIFT) + at * 16 + user_local + 1
    word = jnp.where(at < block_counts[0], word, -1)
    size = -(-(slots + UNROLL) // LANE) * LANE
    word = jnp.pad(word, ((0, size - slots),), constant_values=-1)[None]
    factors = jnp.concatenate([item_factor, item_previous, time_factor, time_previous])
    vmem = pl.BlockSpec(memory_space=pltpu.VMEM)
    hbm = pl.BlockSpec(memory_space=pl.ANY)
    plane = PLANE if n_user % PLANE == 0 else 1
    block_rows = 2 * rows_i + rows_t
    dma = pltpu.SemaphoreType.DMA
    items, times, table = pl.pallas_call(
        functools.partial(gather_kernel, n_user, plane, rows_i),
        out_shape=(
            jax.ShapeDtypeStruct((2, rows_i * n_user, rank), jnp.bfloat16),
            jax.ShapeDtypeStruct((2, rows_t * n_user, rank), jnp.bfloat16),
            jax.ShapeDtypeStruct((8, size), jnp.int32),
        ),
        in_specs=[vmem, vmem],
        out_specs=(vmem,) * 3,
        scratch_shapes=[
            pltpu.VMEM((block_rows, rank), jnp.bfloat16),
            pltpu.VMEM((n_user, block_rows, rank), jnp.bfloat16),
            pltpu.VMEM((n_user, rows_t, rank), jnp.bfloat16),
            dma((n_user // plane,)),
            dma((n_user // plane, plane)),
            dma((n_user,)),
            dma((n_user,)),
            dma((n_user,)),
        ],
        compiler_params=pltpu.CompilerParams(
            collective_id=0, has_side_effects=True, vmem_limit_bytes=16 << 20
        ),
        name="gather",
    )(word, factors)
    part = pl.pallas_call(
        functools.partial(product_kernel, shift),
        out_shape=jax.ShapeDtypeStruct((n_item, 2, U_DEV, rank), jnp.float32),
        in_specs=[hbm, vmem, vmem, vmem],
        out_specs=vmem,
        scratch_shapes=[
            pltpu.VMEM((2, rows_i * n_user // BS, BS * BS, rank), jnp.bfloat16),
            pltpu.SMEM((8, size), jnp.int32),
            dma,
        ]
        + [pltpu.VMEM((range_tiles + 1, BS, rank), jnp.float32)] * (2 * WIDTH),
        compiler_params=pltpu.CompilerParams(vmem_limit_bytes=32 << 20),
        name="products",
    )(table, items, times, blocks)
    return pl.pallas_call(
        finish_kernel,
        out_shape=(
            jax.ShapeDtypeStruct((2, U_DEV, rank), jnp.float32),
            jax.ShapeDtypeStruct((2, rank, rank), jnp.float32),
        ),
        in_specs=[vmem] * 3,
        out_specs=(vmem, vmem),
        scratch_shapes=[
            pltpu.VMEM((2, U_DEV, rank), jnp.float32),
            pltpu.VMEM((2, rows_i * n_user, rank), jnp.bfloat16),
            pltpu.SemaphoreType.DMA((2,)),
            pltpu.SemaphoreType.DMA((2,)),
        ],
        compiler_params=pltpu.CompilerParams(
            collective_id=1, has_side_effects=True, vmem_limit_bytes=32 << 20
        ),
        name="finish",
    )(part, items, times)


def solution(mesh):
    in_specs = (
        P(("groups", "user", "item"), None, None),
        P(("groups", "user", "item")),
        P(("groups", "user", "item")),
        P(("groups", "user", "item")),
        P(("groups", "user", "item")),
        P(("groups", "user", "item"), None),
        P(("groups", "user", "item"), None),
        P(("groups", "user"), None),
        P(("groups", "user"), None),
    )
    out_specs = (P(None, ("groups", "user", "item"), None), P("groups", None, None))
    body = functools.partial(local, mesh.shape["user"], mesh.shape["item"])
    return jax.shard_map(body, mesh=mesh, in_specs=in_specs, out_specs=out_specs, check_vma=False)
```

```python
import functools

import jax
import jax.numpy as jnp
from jax import lax
from jax.experimental import pallas as pl
from jax.experimental.pallas import tpu as pltpu
from jax.sharding import PartitionSpec as P

BS = 16
U_DEV = 64
LANE = 128
WIDTH = 4
UNROLL = 32
SHIFT = 13
PLANE = 4

extrapolation = 0.5


def extended(current, previous):
    wide_now = current.astype(jnp.float32)
    grown = wide_now + extrapolation * (wide_now - previous.astype(jnp.float32))
    return grown.astype(jnp.bfloat16)


def as_columns(row, size):
    parts = []
    for at in range(0, size, LANE):
        square = jnp.broadcast_to(row[:, at : at + LANE], (LANE, LANE))
        parts.append(square.T)
    return jnp.concatenate(parts, axis=0)


def order_slots(word, size):
    down = lax.broadcasted_iota(jnp.int32, (size, LANE), 0)
    across = lax.broadcasted_iota(jnp.int32, (1, LANE), 1)
    key = word >> SHIFT
    key_col = as_columns(key, size)
    places = []
    for at in range(0, size, LANE):
        earlier = (key_col == key[:, at : at + LANE]) & (down < across + at)
        places.append(jnp.sum(earlier.astype(jnp.int32), axis=0, keepdims=True))
    place = jnp.concatenate(places, axis=1)
    return jnp.where(word >= 0, key * size + place, jnp.int32(2**31 - 1)), place


def group_slots(word, order, place, size):
    order_col = as_columns(order, size)
    leads = (order_col & (WIDTH - 1)) == 0
    groups = []
    for at in range(0, size, LANE):
        ahead = leads & (order_col <= order[:, at : at + LANE])
        groups.append(jnp.sum(ahead.astype(jnp.int32), axis=0, keepdims=True))
    group = jnp.concatenate(groups, axis=1) - 1
    spot = jnp.where(word >= 0, group * WIDTH + (place & (WIDTH - 1)), -1)
    return spot, jnp.sum(leads.astype(jnp.int32), axis=0, keepdims=True)


def fill_table(word, spot, total, table_ref, size):
    across = lax.broadcasted_iota(jnp.int32, (1, LANE), 1)
    spot_col = as_columns(spot, size)
    word_col = as_columns(word, size)
    zero = jnp.zeros_like(word_col)
    table_ref[...] = jnp.zeros(table_ref.shape, jnp.int32)
    for at in range(0, size, LANE):
        for m in range(WIDTH):
            here = spot_col == (across + at) * WIDTH + m
            picked = jnp.sum(jnp.where(here, word_col, zero), axis=0, keepdims=True)
            table_ref[m : m + 1, at : at + LANE] = picked
    table_ref[WIDTH : WIDTH + 1, 0:LANE] = total


def flip(index, bits):
    bit = 1
    while bit <= bits:
        if bits & bit:
            index = index + bit - 2 * bit * ((index // bit) % 2)
        bit *= 2
    return index


def gather_kernel(
    n_user, plane, rows_i, word_ref, factors_ref,
    items_ref, times_ref, table_ref, own, held, crossed, line_send, plane_send, cross_send, recv, cross_recv,
):
    lines = n_user // plane
    me, core = lax.axis_index("user"), lax.axis_index("item")
    line, spot = me // plane, me % plane
    rows_t = factors_ref.shape[0] // 2 - rows_i
    barrier = pltpu.get_barrier_semaphore()

    def to(user):
        return {"user": user}

    line_peers = [flip(line, d) * plane + spot for d in range(1, lines)]
    plane_peers = [line * plane + flip(spot, d) for d in range(1, plane)]
    for peer in line_peers + plane_peers:
        pl.semaphore_signal(barrier, inc=1, device_id=to(peer), device_id_type=pl.DeviceIdType.MESH)
    pl.semaphore_signal(barrier, inc=1, device_id={"item": 1 - core}, device_id_type=pl.DeviceIdType.MESH)
    item, time = factors_ref[0:rows_i], factors_ref[2 * rows_i : 2 * rows_i + rows_t]
    item_new = extended(item, factors_ref[rows_i : 2 * rows_i])
    time_new = extended(time, factors_ref[2 * rows_i + rows_t :])
    own[0:rows_i] = item
    own[rows_i : 2 * rows_i] = item_new
    first = jnp.broadcast_to(core, time.shape) == 0
    own[2 * rows_i :] = jnp.where(first, time.astype(jnp.float32), time_new.astype(jnp.float32)).astype(jnp.bfloat16)
    pl.semaphore_wait(barrier, lines + plane - 1)

    def copy(src, dst, send, receive, device):
        return pltpu.make_async_remote_copy(
            src_ref=src, dst_ref=dst, send_sem=send, recv_sem=receive,
            device_id=device, device_id_type=pl.DeviceIdType.MESH,
        )

    sends = []
    for d in range(1, lines):
        sends.append(copy(own, held.at[me], line_send.at[d], recv.at[me], to(line_peers[d - 1])))
    for d in range(1, plane):
        sends.append(copy(own, held.at[me], plane_send.at[0, d], recv.at[me], to(plane_peers[d - 1])))
    for send in sends:
        send.start()

    def arrive(source):
        copy(held.at[source], held.at[source], line_send.at[0], recv.at[source], to(source)).wait_recv()

    def across(source, n):
        return copy(
            held.at[source, pl.ds(2 * rows_i, rows_t)], crossed.at[source],
            cross_send.at[n], cross_recv.at[source], {"item": 1 - core},
        )

    def forward(d):
        source = line_peers[d - 1]
        arrive(source)
        for e in range(1, plane):
            sends.append(copy(held.at[source], held.at[source], plane_send.at[d, e], recv.at[source], to(plane_peers[e - 1])))
            sends[-1].start()
        sends.append(across(source, d * plane))
        sends[-1].start()

    size = word_ref.shape[1]
    word = word_ref[...]
    order, place = order_slots(word, size)
    if lines > 1:
        forward(1)
    slot, total = group_slots(word, order, place, size)
    for d in range(2, lines):
        forward(d)
    fill_table(word, slot, total, table_ref, size)

    def put(source, block):
        at_i = pl.multiple_of(source * rows_i, rows_i)
        at_t = pl.multiple_of(source * rows_t, rows_t)
        for s in range(2):
            items_ref[s, pl.ds(at_i, rows_i)] = block[s * rows_i : (s + 1) * rows_i]
        times_ref[core, pl.ds(at_t, rows_t)] = block[2 * rows_i :]

    at_me = pl.multiple_of(me * rows_t, rows_t)
    times_ref[0, pl.ds(at_me, rows_t)] = time
    times_ref[1, pl.ds(at_me, rows_t)] = time_new
    for s, rows in enumerate((item, item_new)):
        items_ref[s, pl.ds(pl.multiple_of(me * rows_i, rows_i), rows_i)] = rows
    sources = [(d * plane, line_peers[d - 1]) for d in range(1, lines)]
    for d in range(lines):
        for e in range(1, plane):
            source = flip(line, d) * plane + flip(spot, e)
            arrive(source)
            sends.append(across(source, d * plane + e))
            sends[-1].start()
            sources.append((d * plane + e, source))
    for n, source in sources:
        put(source, held.at[source])
    for n, source in sources:
        across(source, n).wait_recv()
        at_t = pl.multiple_of(source * rows_t, rows_t)
        times_ref[1 - core, pl.ds(at_t, rows_t)] = crossed[source]
    for send in sends:
        send.wait_send()


def product_kernel(
    shift, table_hbm, items_ref, times_ref, tensor, part_ref, spread, table_ref, table_sem, *totals
):
    rank = items_ref.shape[2]
    plan = pltpu.make_async_copy(table_hbm, table_ref, table_sem)
    plan.start()
    for total in totals:
        total[...] = jnp.zeros_like(total)

    def widen(tile, carry):
        at = pl.multiple_of(tile * BS, BS)
        for s in range(2):
            rows = items_ref[s, pl.ds(at, BS)].astype(jnp.float32)
            for j in range(BS):
                wide = jnp.broadcast_to(rows[j : j + 1], (BS, rank))
                spread[s, tile, j * BS : (j + 1) * BS] = wide.astype(jnp.bfloat16)
        return carry

    lax.fori_loop(0, items_ref.shape[1] // BS, widen, 0)
    plan.wait()
    count = table_ref[WIDTH, 0]

    def turn(g, carry):
        for v in range(UNROLL):
            c = g * UNROLL + v
            member = [table_ref[m, c] for m in range(WIDTH)]
            key = member[0] >> SHIFT
            tile = key >> shift
            at = pl.multiple_of((key & ((1 << shift) - 1)) * BS, BS)
            x = jnp.concatenate([tensor[(word >> 4) & 511] for word in member], axis=0)
            for s in range(2):
                right = times_ref[s, pl.ds(at, BS)]
                left = spread[s, tile].reshape(BS, BS, rank)
                khatri = (left * right[None]).reshape(BS * BS, rank)
                y = jnp.dot(x, khatri, preferred_element_type=jnp.float32)
                for m, word in enumerate(member):
                    totals[m * 2 + s][word & 15] += y[m * BS : (m + 1) * BS]
        return carry

    lax.fori_loop(0, (count + UNROLL - 1) // UNROLL, turn, 0)
    tiles = U_DEV // BS
    for half in range(part_ref.shape[0]):
        for s in range(2):
            for n in range(tiles):
                part_ref[half, s, n * BS : (n + 1) * BS] = sum(
                    totals[m * 2 + s][1 + half * tiles + n] for m in range(WIDTH)
                )


def gram(rows):
    return lax.dot_general(rows, rows, (((0,), (0,)), ((), ())), preferred_element_type=jnp.float32)


def finish_kernel(part_ref, items_ref, times_ref, rows_ref, grams_ref, theirs, items, send_sem, recv_sem):
    me = lax.axis_index("item")
    other = 1 - me
    barrier = pltpu.get_barrier_semaphore()
    pl.semaphore_signal(barrier, inc=1, device_id={"item": other}, device_id_type=pl.DeviceIdType.MESH)
    pl.semaphore_wait(barrier, 1)
    copies = []
    for n, (src, dst) in enumerate(((part_ref.at[other], theirs), (items_ref, items))):
        copies.append(
            pltpu.make_async_remote_copy(
                src_ref=src, dst_ref=dst, send_sem=send_sem.at[n], recv_sem=recv_sem.at[n],
                device_id={"item": other}, device_id_type=pl.DeviceIdType.MESH,
            )
        )
        copies[-1].start()
    mine = [gram(items_ref[s]) for s in range(2)]
    times = [gram(times_ref[s]) for s in range(2)]
    copies[0].wait()
    rows_ref[...] = part_ref[me] + theirs[...]
    copies[1].wait()
    for s in range(2):
        grams_ref[s] = (mine[s] + gram(items[s])) * times[s]


def local(
    n_user, n_item, blocks, user_blocks, item_blocks, time_blocks, block_counts,
    item_factor, item_previous, time_factor, time_previous,
):
    slots, _, width = blocks.shape
    rank = item_factor.shape[1]
    rows_i, rows_t = item_factor.shape[0], time_factor.shape[0]
    range_tiles = U_DEV * n_item // BS
    per_shard = rows_i // BS
    shift = (rows_t * n_user // BS - 1).bit_length()
    user_local = user_blocks - lax.axis_index("user") * range_tiles
    item_local = item_blocks // per_shard // n_item * per_shard + item_blocks % per_shard
    at = jnp.arange(slots, dtype=jnp.int32)
    word = (((item_local << shift) + time_blocks) << SHIFT) + at * 16 + user_local + 1
    word = jnp.where(at < block_counts[0], word, -1)
    size = -(-(slots + UNROLL) // LANE) * LANE
    word = jnp.pad(word, ((0, size - slots),), constant_values=-1)[None]
    factors = jnp.concatenate([item_factor, item_previous, time_factor, time_previous])
    vmem = pl.BlockSpec(memory_space=pltpu.VMEM)
    hbm = pl.BlockSpec(memory_space=pl.ANY)
    plane = PLANE if n_user % PLANE == 0 else 1
    block_rows = 2 * rows_i + rows_t
    dma = pltpu.SemaphoreType.DMA
    items, times, table = pl.pallas_call(
        functools.partial(gather_kernel, n_user, plane, rows_i),
        out_shape=(
            jax.ShapeDtypeStruct((2, rows_i * n_user, rank), jnp.bfloat16),
            jax.ShapeDtypeStruct((2, rows_t * n_user, rank), jnp.bfloat16),
            jax.ShapeDtypeStruct((8, size), jnp.int32),
        ),
        in_specs=[vmem, vmem],
        out_specs=(vmem,) * 3,
        scratch_shapes=[
            pltpu.VMEM((block_rows, rank), jnp.bfloat16),
            pltpu.VMEM((n_user, block_rows, rank), jnp.bfloat16),
            pltpu.VMEM((n_user, rows_t, rank), jnp.bfloat16),
            dma((n_user // plane,)),
            dma((n_user // plane, plane)),
            dma((n_user,)),
            dma((n_user,)),
            dma((n_user,)),
        ],
        compiler_params=pltpu.CompilerParams(
            collective_id=0, has_side_effects=True, vmem_limit_bytes=16 << 20
        ),
        name="gather",
    )(word, factors)
    part = pl.pallas_call(
        functools.partial(product_kernel, shift),
        out_shape=jax.ShapeDtypeStruct((n_item, 2, U_DEV, rank), jnp.float32),
        in_specs=[hbm, vmem, vmem, vmem],
        out_specs=vmem,
        scratch_shapes=[
            pltpu.VMEM((2, rows_i * n_user // BS, BS * BS, rank), jnp.bfloat16),
            pltpu.SMEM((8, size), jnp.int32),
            dma,
        ]
        + [pltpu.VMEM((range_tiles + 1, BS, rank), jnp.float32)] * (2 * WIDTH),
        compiler_params=pltpu.CompilerParams(vmem_limit_bytes=32 << 20),
        name="products",
    )(table, items, times, blocks)
    return pl.pallas_call(
        finish_kernel,
        out_shape=(
            jax.ShapeDtypeStruct((2, U_DEV, rank), jnp.float32),
            jax.ShapeDtypeStruct((2, rank, rank), jnp.float32),
        ),
        in_specs=[vmem] * 3,
        out_specs=(vmem, vmem),
        scratch_shapes=[
            pltpu.VMEM((2, U_DEV, rank), jnp.float32),
            pltpu.VMEM((2, rows_i * n_user, rank), jnp.bfloat16),
            pltpu.SemaphoreType.DMA((2,)),
            pltpu.SemaphoreType.DMA((2,)),
        ],
        compiler_params=pltpu.CompilerParams(
            collective_id=1, has_side_effects=True, vmem_limit_bytes=32 << 20
        ),
        name="finish",
    )(part, items, times)


def solution(mesh):
    in_specs = (
        P(("groups", "user", "item"), None, None),
        P(("groups", "user", "item")),
        P(("groups", "user", "item")),
        P(("groups", "user", "item")),
        P(("groups", "user", "item")),
        P(("groups", "user", "item"), None),
        P(("groups", "user", "item"), None),
        P(("groups", "user"), None),
        P(("groups", "user"), None),
    )
    out_specs = (P(None, ("groups", "user", "item"), None), P("groups", None, None))
    body = functools.partial(local, mesh.shape["user"], mesh.shape["item"])
    return jax.shard_map(body, mesh=mesh, in_specs=in_specs, out_specs=out_specs, check_vma=False)
```
